32 devices in a mesh: head: 4 (over z), blk: 8 (over y, x, core).
Axes of the slice: x: 2, y: 2, z: 4, core: 2. Of those that a mesh axis runs over, the one named last changes fastest.
Arguments:
- hidden: bfloat16 [2, 2048, 768], P(None, ('head', 'blk')), may hold values from -6 to 6
- entity_flags: int32 [2, 2048], P(None, ('head', 'blk')), may hold values 0 or 1
- doc_lengths: int32 [2, 32], replicated, may hold values from 1 to 1024, 2048 in all within a row
- cotangent: bfloat16 [2, 2048, 768], P(None, ('head', 'blk')), may hold values from -6 to 6
- query_weight: bfloat16 [2359296], P(('head', 'blk')), may hold values from -0.375 to 0.375
- query_bias: bfloat16 [4, 768], replicated, may hold values from -4 to 4
- keyval_weight: bfloat16 [1179648], P(('head', 'blk')), may hold values from -0.375 to 0.375
- value_bias: bfloat16 [768], replicated, may hold values from -6 to 6
- output_weight: bfloat16 [589824], P(('head', 'blk')), may hold values from -0.21875 to 0.21875
- output_bias: bfloat16 [768], replicated, may hold values from -6 to 6
- first_gain: bfloat16 [768], replicated, may hold values from 0.5 to 1.5
- first_shift: bfloat16 [768], replicated, may hold values from -4 to 4
- inner_weight: bfloat16 [2359296], P(('head', 'blk')), may hold values from -0.21875 to 0.21875
- inner_bias: bfloat16 [3072], replicated, may hold values from -6 to 6
- outer_weight: bfloat16 [2359296], P(('head', 'blk')), may hold values from -0.109375 to 0.109375
- outer_bias: bfloat16 [768], replicated, may hold values from -6 to 6
- second_gain: bfloat16 [768], replicated, may hold values from 0.5 to 1.5
- second_shift: bfloat16 [768], replicated, may hold values from -4 to 4
Outputs:
- layer_output: bfloat16 [2, 2048, 768], P(None, ('head', 'blk'))
- grad_hidden: float32 [2, 2048, 768], P(None, ('head', 'blk'))
- grad_query_weight: float32 [2359296], P(('head', 'blk'))
- grad_query_bias: float32 [4, 768], replicated
- grad_keyval_weight: float32 [1179648], P(('head', 'blk'))
- grad_value_bias: float32 [768], replicated
- grad_output_weight: float32 [589824], P(('head', 'blk'))
- grad_output_bias: float32 [768], replicated
- grad_first_gain: float32 [768], replicated
- grad_first_shift: float32 [768], replicated
- grad_inner_weight: float32 [2359296], P(('head', 'blk'))
- grad_inner_bias: float32 [3072], replicated
- grad_outer_weight: float32 [2359296], P(('head', 'blk'))
- grad_outer_bias: float32 [768], replicated
- grad_second_gain: float32 [768], replicated
- grad_second_shift: float32 [768], replicated
The draws below stay inside these ranges and needn't reach their ends.
Inputs may be any that keep to these rules, and one draw needn't show every extreme that they name: `doc_lengths`: each row holds the lengths of 32 documents that fill the sequence end to end in this order; the longest has exactly 1024 tokens. `entity_flags`: 1 marks an entity token, 0 a word token.
All inputs are finite; a program needn't handle non-finite values. No bound on the sum of `entity_flags` on one device may be relied on, other than what follows from the above.
Results may differ from the reference program's by a relative error of at most 0.023.
Values may be sent and summed in bfloat16 or wider, within the bound.
No kernel may reach another device: no remote copies, remote signals or barrier semaphores. Data moves between devices by JAX's collectives and lax.ppermute only.
A program may use at most 256 MiB of HBM per device.

```python
import math
import jax
import jax.numpy as jnp
import numpy as np
from jax import lax

D = 768
HEADS = 12
HD = 64
FF = 3072
MICRO = 2
NDOCS = 32
LEN = 2048


def touch_ends(drawn, key, low, largest):
    index_at = [jax.random.randint(jax.random.fold_in(key, axis), (), 0, length) for axis, length in enumerate(drawn.shape)]
    main_axis = drawn.shape.index(max(drawn.shape))
    next_to = index_at[:main_axis] + [(index_at[main_axis] + 1) % drawn.shape[main_axis]] + index_at[main_axis + 1:]
    return drawn.at[tuple(index_at)].set(low).at[tuple(next_to)].set(largest)


def level_of(stream_key, dims, pieces, low, largest):
    loudness, own = 1.0, jax.random.fold_in(stream_key, 6)
    for axis_at, shards_of in pieces:
        draws = jnp.exp(jax.random.uniform(jax.random.fold_in(own, axis_at), (shards_of,), jnp.float32, low / len(pieces), largest / len(pieces)))
        loudness = loudness * jnp.repeat(draws, dims[axis_at] // shards_of).reshape([-1 if axis == axis_at else 1 for axis in range(len(dims))])
    return loudness


def profile(amount, total, most, lean):
    weights = [(1 << 20) // math.isqrt(grade ** lean) + 1 for grade in range(2, amount + 1)]
    rest, given = total - most - (amount - 1), [1] * (amount - 1)
    while rest > 0:
        free = [i for i in range(amount - 1) if given[i] < most]
        mass, remaining = sum([weights[i] for i in free]), rest
        for i in free:
            more = min(most - given[i], max(1, remaining * weights[i] // mass), rest)
            given[i] = given[i] + more
            rest = rest - more
    return np.array([most] + given)


def ragged_sizes(rng, number_of, total, limit, lean):
    if number_of == 2:
        one = jax.random.randint(rng, (), max(1, total - limit), min(limit, total - 1) + 1)
        return jnp.stack([one, total - one])
    sizes = jnp.asarray(profile(number_of, total, limit, lean), jnp.int32)
    twos = (number_of - 1) // 2
    giver, taker = sizes[1:1 + 2 * twos:2], sizes[2:2 + 2 * twos:2]
    room = jnp.minimum(giver - 1, limit - taker)
    moved = jax.random.randint(jax.random.fold_in(rng, 1), (twos,), 0, 1 << 20) % (room + 1)
    sizes = sizes.at[1:1 + 2 * twos:2].set(giver - moved).at[2:2 + 2 * twos:2].set(taker + moved)
    return sizes[jax.random.permutation(jax.random.fold_in(rng, 2), number_of)]


def normal_values(key, dims, scale, bound, pieces=(), held_as=jnp.bfloat16):
    values = jax.random.normal(key, dims, jnp.float32) * scale
    if len(pieces) > 0:
        values = level_of(key, dims, pieces, -0.22, 0.18) * values
    return jnp.clip(values, min=-bound, max=bound).astype(held_as)


def setup_inputs(seed: int = 0) -> dict:
    splits = jax.random.split(jax.random.key(seed), 19)
    return {
        "hidden": normal_values(splits[0], (MICRO, LEN, D), 1.0, 6.0, ((1, 32),)),
        "entity_flags": touch_ends((jax.random.randint(splits[1], (MICRO, LEN), 0, 4) < 1).astype(jnp.int32), jax.random.fold_in(splits[1], 1), 0, 1),
        "doc_lengths": jax.vmap(lambda own: ragged_sizes(own, NDOCS, LEN, LEN // 2, 2))(jax.random.split(splits[2], MICRO)).reshape((MICRO, NDOCS)).astype(jnp.int32),
        "cotangent": normal_values(splits[3], (MICRO, LEN, D), 1.0, 6.0, ((1, 32),)),
        "query_weight": normal_values(splits[4], (4 * D * D,), (D // 3) ** -0.5, 0.375, ((0, 32),)),
        "query_bias": normal_values(splits[5], (4, D), 0.3, 4.0),
        "keyval_weight": normal_values(splits[6], (2 * D * D,), (D // 3) ** -0.5, 0.375, ((0, 32),)),
        "value_bias": normal_values(splits[7], (D,), 0.5, 6.0),
        "output_weight": normal_values(splits[8], (D * D,), D ** -0.5, 0.21875, ((0, 32),)),
        "output_bias": normal_values(splits[9], (D,), 0.5, 6.0),
        "first_gain": jnp.clip(1.0 + 0.1 * jax.random.normal(splits[10], (D,), jnp.float32), 0.5, 1.5).astype(jnp.bfloat16),
        "first_shift": normal_values(splits[11], (D,), 0.3, 4.0),
        "inner_weight": normal_values(splits[12], (D * FF,), D ** -0.5, 0.21875, ((0, 32),)),
        "inner_bias": normal_values(splits[13], (FF,), 0.5, 6.0),
        "outer_weight": normal_values(splits[14], (FF * D,), FF ** -0.5, 0.109375, ((0, 32),)),
        "outer_bias": normal_values(splits[15], (D,), 0.5, 6.0),
        "second_gain": jnp.clip(1.0 + 0.1 * jax.random.normal(splits[16], (D,), jnp.float32), 0.5, 1.5).astype(jnp.bfloat16),
        "second_shift": normal_values(splits[17], (D,), 0.3, 4.0),
    }


@jax.custom_vjp
def low(v):
    return lax.optimization_barrier(v.astype(jnp.bfloat16)).astype(jnp.float32)

@jax.custom_vjp
def low_back(v):
    return v

def low_keep(v):
    return (low(v), None)

def low_pass(kept, grad):
    return (grad,)

def back_keep(v):
    return (v, None)

def back_low(kept, grad):
    return (low(grad),)
low.defvjp(low_keep, low_pass)
low_back.defvjp(back_keep, back_low)
top_precision = lax.Precision.HIGHEST
norm_eps = 1e-12

def layer_norm(values, gain, shift):
    centre = lax.optimization_barrier(jnp.mean(values, -1, keepdims=True))
    centred = values - centre
    return centred * lax.rsqrt(lax.optimization_barrier(jnp.mean(centred * centred, -1, keepdims=True)) + norm_eps) * gain + shift

def attention(queries, wide_keys, values, documents):
    block_rows = min(256, LEN)
    block_count = LEN // block_rows
    score_scale = 1.0 / math.sqrt(HD)

    def one_block(block_items):
        query_block, document_block = block_items
        scores = low_back(jnp.einsum('qhd,khd->hqk', query_block, wide_keys, precision=top_precision) * score_scale)
        same_document = document_block[:, None] == documents[None, :]
        scores = jnp.where(same_document[None], scores, -jnp.inf)
        highest = lax.optimization_barrier(jnp.max(scores, -1, keepdims=True))
        log_total = highest + jnp.log(lax.optimization_barrier(jnp.sum(jnp.exp(scores - highest), -1, keepdims=True)))
        weights = low(jnp.exp(scores - log_total))
        return jnp.einsum('hqk,khd->qhd', weights, values, precision=top_precision)
    blocks = (queries.reshape(block_count, block_rows, HEADS, 2 * HD), documents.reshape(block_count, block_rows))
    return lax.map(jax.checkpoint(one_block), blocks).reshape(LEN, HEADS, HD)

def layer(inputs, flags, lengths, query_weight, query_bias, keyval_weight, value_bias, output_weight, output_bias, first_gain, first_shift, inner_weight, inner_bias, outer_weight, outer_bias, second_gain, second_shift):
    positions = jnp.arange(LEN, dtype=jnp.int32)
    documents = lax.optimization_barrier(jnp.sum((jnp.cumsum(lengths)[None, :] <= positions[:, None]).astype(jnp.int32), 1))
    entity_mask = (flags == 1)[:, None]
    projected = jnp.einsum('td,dke->tke', inputs, query_weight.reshape(D, 4, D), precision=top_precision) + query_bias
    toward_words = jnp.where(entity_mask, projected[:, 2], projected[:, 0]).reshape(LEN, HEADS, HD)
    toward_entities = jnp.where(entity_mask, projected[:, 3], projected[:, 1]).reshape(LEN, HEADS, HD)
    queries = low_back(low(jnp.concatenate([toward_words, toward_entities], -1)))
    paired = jnp.einsum('td,dke->tke', inputs, keyval_weight.reshape(D, 2, D), precision=top_precision)
    keys = low_back(low(paired[:, 0].reshape(LEN, HEADS, HD)))
    values = low_back(low((paired[:, 1] + value_bias).reshape(LEN, HEADS, HD)))
    entity_share = flags.astype(inputs.dtype)[:, None, None]
    wide_keys = jnp.concatenate([keys * (1 - entity_share), keys * entity_share], -1)
    context = low_back(low(attention(queries, wide_keys, values, documents))).reshape(LEN, D)
    attended = low_back(jnp.dot(context, output_weight.reshape(D, D), precision=top_precision) + output_bias)
    first = layer_norm(inputs + attended, first_gain, first_shift)
    inner = low_back(jnp.dot(low(first), inner_weight.reshape(D, FF), precision=top_precision) + inner_bias)
    outer = low_back(jnp.dot(low(jax.nn.gelu(inner)), outer_weight.reshape(FF, D), precision=top_precision) + outer_bias)
    return layer_norm(first + outer, second_gain, second_shift)

def reference(hidden, entity_flags, doc_lengths, cotangent, query_weight, query_bias, keyval_weight, value_bias, output_weight, output_bias, first_gain, first_shift, inner_weight, inner_bias, outer_weight, outer_bias, second_gain, second_shift):
    weights = (query_weight.astype(jnp.float32), query_bias.astype(jnp.float32), keyval_weight.astype(jnp.float32), value_bias.astype(jnp.float32), output_weight.astype(jnp.float32), output_bias.astype(jnp.float32), first_gain.astype(jnp.float32), first_shift.astype(jnp.float32), inner_weight.astype(jnp.float32), inner_bias.astype(jnp.float32), outer_weight.astype(jnp.float32), outer_bias.astype(jnp.float32), second_gain.astype(jnp.float32), second_shift.astype(jnp.float32))

    def whole(inputs, *params):

        def one_micro(micro_items):
            return layer(micro_items[0], micro_items[1], micro_items[2], *params)
        return lax.map(one_micro, (inputs, entity_flags, doc_lengths))
    result, pullback = jax.vjp(whole, hidden.astype(jnp.float32), *weights)
    gradients = pullback(cotangent.astype(jnp.float32))
    return (result.astype(jnp.bfloat16), gradients[0], gradients[1], gradients[2], gradients[3], gradients[4], gradients[5], gradients[6], gradients[7], gradients[8], gradients[9], gradients[10], gradients[11], gradients[12], gradients[13], gradients[14])
```

```python
import math

import jax
import jax.numpy as jnp
from jax import lax
from jax.experimental import pallas as pl
from jax.experimental.pallas import tpu as pltpu
from jax.sharding import PartitionSpec as P

HEADS = 12
HD = 64
WIDE = 2 * HD
EPS = 1e-12
GELU_A = math.sqrt(2.0 / math.pi)
GELU_B = 0.044715
F32 = jnp.float32
BF16 = jnp.bfloat16
NEG = -1e30
VMEM_BYTES = 58 * 1024 * 1024


def any_spec():
    return pl.BlockSpec(memory_space=pl.ANY)


def vmem_spec():
    return pl.BlockSpec(memory_space=pltpu.VMEM)


def smem_spec():
    return pl.BlockSpec(memory_space=pltpu.SMEM)


def dot(a, b):
    return lax.dot_general(a, b, (((1,), (0,)), ((), ())), preferred_element_type=F32)


def dot_tn(a, b):
    return lax.dot_general(a, b, (((0,), (0,)), ((), ())), preferred_element_type=F32)


def dot_nt(a, b):
    return lax.dot_general(a, b, (((1,), (1,)), ((), ())), preferred_element_type=F32)


def project_kernel(groups, heads, w_col, place, x_refs, w_hbm, bias, flag, q_out, kv_out, x_out, w, sem):
    rows = x_refs[0].shape[0]
    cols = w.shape[1]
    half = heads * WIDE
    copy = pltpu.make_async_copy(
        w_hbm.at[:, pl.ds(pl.multiple_of(w_col + place[0] * cols, 128), cols)], w, sem
    )
    copy.start()
    copy.wait()
    for step in range(groups):
        seg = lax.rem(place[0] + (groups - step), groups)
        x = x_refs[step][...]
        x_out[seg] = x
        y = dot(x, w[...]) + bias[...]
        entity = flag[seg] == 1.0
        for h in range(heads):
            word = y[:, h * WIDE : (h + 1) * WIDE]
            ent = y[:, half + h * WIDE : half + (h + 1) * WIDE]
            q_out[h, seg] = jnp.where(entity, ent, word).astype(BF16)
            kv_out[h, seg] = y[:, 2 * half + h * WIDE : 2 * half + (h + 1) * WIDE].astype(BF16)


def project(place, xs, w, bias, flag, heads):
    groups = len(xs)
    rows, width = xs[0].shape
    cols = bias.shape[1]

    def kernel(place_ref, *refs):
        x_refs = refs[:groups]
        project_kernel(groups, heads, 0, place_ref, x_refs, *refs[groups:])

    return pl.pallas_call(
        kernel,
        out_shape=(
            jax.ShapeDtypeStruct((heads, groups, rows, WIDE), BF16),
            jax.ShapeDtypeStruct((heads, groups, rows, WIDE), BF16),
            jax.ShapeDtypeStruct((groups, rows, width), BF16),
        ),
        in_specs=[smem_spec()] + [vmem_spec()] * groups + [any_spec(), vmem_spec(), vmem_spec()],
        out_specs=(vmem_spec(), vmem_spec(), vmem_spec()),
        scratch_shapes=[pltpu.VMEM((width, cols), BF16), pltpu.SemaphoreType.DMA],
        compiler_params=pltpu.CompilerParams(vmem_limit_bytes=VMEM_BYTES),
        cost_estimate=pl.CostEstimate(
            flops=2 * groups * rows * width * cols, bytes_accessed=4 * width * cols, transcendentals=0
        ),
        name="project",
    )(place, *xs, w, bias, flag)


def flag_of(code):
    code = code.astype(F32)
    return code - 2.0 * jnp.floor(0.5 * code)


def chunk_of(length):
    return min(512, length)


def attend_kernel(
    groups, heads, blocks, place, span, q, *refs
):
    kv_pieces = refs[:blocks]
    code_k, doc_q = refs[blocks : blocks + 2]
    ctx_out, lse_out, kv_out, wk_out = refs[blocks + 2 : blocks + 6]
    kv_sem = refs[blocks + 6]
    rows = q.shape[2]
    length = groups * blocks * rows
    chunk = chunk_of(length)
    scale = 1.0 / math.sqrt(HD)
    copies = []
    for p in range(blocks):
        at = place[1] ^ p
        for h in range(heads):
            for g in range(groups):
                start = pl.multiple_of((g * blocks + at) * rows, rows)
                copies.append(
                    pltpu.make_async_copy(
                        kv_pieces[p].at[h, g], kv_out.at[h, pl.ds(start, rows)], kv_sem
                    )
                )
    for c in copies:
        c.start()
    for c in copies:
        c.wait()
    lane = lax.broadcasted_iota(jnp.int32, (1, WIDE), 1) < HD

    def widen(i, _):
        at = pl.ds(pl.multiple_of(i * chunk, chunk), chunk)
        flag = flag_of(code_k[at, :])
        share = jnp.where(lane, 1.0 - flag, flag)
        for h in range(heads):
            kv = kv_out[h, at, :].astype(F32)
            both = jnp.where(lane, kv, pltpu.roll(kv, HD, 1))
            wk_out[h, at, :] = (both * share).astype(BF16)
        return 0

    lax.fori_loop(0, length // chunk, widen, 0)

    for seg in range(groups):
        dq = 2.0 * doc_q[seg : seg + 1, :] + 0.5
        qt = [q[h, seg].T for h in range(heads)]

        def step(i, carry):
            at = pl.ds(pl.multiple_of(i * chunk, chunk), chunk)
            same = jnp.abs(code_k[at, :].astype(F32) - dq) < 1.0
            out = []
            for h in range(heads):
                m, l, acc = carry[h]
                s = dot(wk_out[h, at, :], qt[h]) * scale
                s = jnp.where(same, s, NEG)
                m_new = jnp.maximum(m, jnp.max(s, 0, keepdims=True))
                factor = jnp.exp(m - m_new)
                p = jnp.exp(s - m_new)
                l = l * factor + jnp.sum(p, 0, keepdims=True)
                acc = acc * factor + dot_tn(kv_out[h, at, :], p.astype(BF16))
                out.append((m_new, l, acc))
            return tuple(out)

        start = tuple(
            (jnp.full((1, rows), NEG, F32), jnp.zeros((1, rows), F32), jnp.zeros((WIDE, rows), F32))
            for _ in range(heads)
        )
        done = lax.fori_loop(span[seg, 0], span[seg, 1], step, start)
        parts = []
        for h in range(heads):
            m, l, acc = done[h]
            lse_out[seg * heads + h : seg * heads + h + 1, :] = m + jnp.log(l)
            parts.append(acc[HD:, :] / l)
        ctx_out[seg] = jnp.concatenate(parts, 0).T.astype(BF16)


def attend(place, span, q, pieces, code_k, doc_q):
    heads, groups, rows, _ = q.shape
    blocks = len(pieces)
    length = groups * blocks * rows
    flops = 4 * heads * groups * rows * length * WIDE // 2

    def kernel(place_ref, span_ref, q_ref, *refs):
        attend_kernel(groups, heads, blocks, place_ref, span_ref, q_ref, *refs)

    return pl.pallas_call(
        kernel,
        out_shape=(
            jax.ShapeDtypeStruct((groups, rows, heads * HD), BF16),
            jax.ShapeDtypeStruct((groups * heads, rows), F32),
            jax.ShapeDtypeStruct((heads, length, WIDE), BF16),
            jax.ShapeDtypeStruct((heads, length, WIDE), BF16),
        ),
        in_specs=[smem_spec(), smem_spec(), vmem_spec()]
        + [any_spec()] * blocks
        + [vmem_spec()] * 2,
        out_specs=(vmem_spec(), vmem_spec(), vmem_spec(), vmem_spec()),
        scratch_shapes=[pltpu.SemaphoreType.DMA],
        compiler_params=pltpu.CompilerParams(vmem_limit_bytes=VMEM_BYTES),
        cost_estimate=pl.CostEstimate(
            flops=flops, bytes_accessed=4 * heads * length * WIDE, transcendentals=0
        ),
        name="attend",
    )(place, span, q, *pieces, code_k, doc_q)


def attend_back_kernel(
    groups, heads, blocks, place, span, q, kv, wk, ctx, lse, code_k, doc_q, *refs
):
    dctx = refs[:groups]
    dq_out, dkv_out, acc, stage, sem = refs[groups:]
    rows = q.shape[2]
    length = kv.shape[1]
    chunk = chunk_of(length)
    scale = 1.0 / math.sqrt(HD)
    lane = lax.broadcasted_iota(jnp.int32, (1, WIDE), 1) < HD

    def clear(i, _):
        at = pl.ds(pl.multiple_of(i * chunk, chunk), chunk)
        for h in range(heads):
            acc[h, at, :] = jnp.zeros((chunk, WIDE), F32)
        return 0

    lax.fori_loop(0, length // chunk, clear, 0)

    for step_of in range(groups):
        seg = lax.rem(place[0] + (groups - step_of), groups)
        d_t = dctx[step_of][...].astype(F32).T
        c_t = ctx[seg].astype(F32).T
        prod = d_t * c_t
        dq_row = 2.0 * doc_q[pl.ds(seg, 1), :] + 0.5
        qs, qt, d_pad_t, d_pad, deltas, lses = [], [], [], [], [], []
        for h in range(heads):
            qh = q[h, seg]
            qs.append(qh)
            qt.append(qh.T)
            padded = jnp.concatenate(
                [jnp.zeros((HD, rows), F32), d_t[h * HD : (h + 1) * HD, :]], 0
            )
            d_pad_t.append(padded.astype(BF16))
            d_pad.append(padded.T.astype(BF16))
            deltas.append(jnp.sum(prod[h * HD : (h + 1) * HD, :], 0, keepdims=True))
            lses.append(lse[pl.ds(seg * heads + h, 1), :])

        def step(i, carry):
            at = pl.ds(pl.multiple_of(i * chunk, chunk), chunk)
            code = code_k[at, :].astype(F32)
            same = jnp.abs(code - dq_row) < 1.0
            flag = flag_of(code)
            share = jnp.where(lane, 1.0 - flag, flag) * scale
            out = []
            for h in range(heads):
                wide = wk[h, at, :]
                s = dot(wide, qt[h]) * scale
                p = jnp.exp(jnp.where(same, s, NEG) - lses[h])
                dp = dot(kv[h, at, :], d_pad_t[h])
                ds = (p * (dp - deltas[h])).astype(BF16)
                dv = dot(p.astype(BF16), d_pad[h])
                dw = dot(ds, qs[h]) * share
                acc[h, at, :] += jnp.where(lane, dw + pltpu.roll(dw, HD, 1), dv)
                out.append(carry[h] + dot_tn(wide, ds))
            return tuple(out)

        done = lax.fori_loop(
            span[seg, 0],
            span[seg, 1],
            step,
            tuple(jnp.zeros((WIDE, rows), F32) for _ in range(heads)),
        )
        for h in range(heads):
            dq_out[h, seg] = (done[h].T * scale).astype(BF16)

    def out_copy(p):
        return pltpu.make_async_copy(stage.at[p % 2], dkv_out.at[p], sem.at[p % 2])

    for p in range(blocks):
        at = place[1] ^ p
        if p >= 2:
            out_copy(p - 2).wait()
        for h in range(heads):
            for g in range(groups):
                start = pl.multiple_of((g * blocks + at) * rows, rows)
                stage[p % 2, h, g] = acc[h, pl.ds(start, rows), :].astype(BF16)
        out_copy(p).start()
    for p in range(max(0, blocks - 2), blocks):
        out_copy(p).wait()


def attend_back(place, span, q, kv, wk, ctx, lse, code_k, doc_q, dctx):
    heads, groups, rows, _ = q.shape
    length = kv.shape[1]
    blocks = length // (groups * rows)

    def kernel(place_ref, span_ref, *refs):
        attend_back_kernel(groups, heads, blocks, place_ref, span_ref, *refs)

    return pl.pallas_call(
        kernel,
        out_shape=(
            jax.ShapeDtypeStruct((heads, groups, rows, WIDE), BF16),
            jax.ShapeDtypeStruct((blocks, heads, groups, rows, WIDE), BF16),
        ),
        in_specs=[smem_spec(), smem_spec()] + [vmem_spec()] * (7 + groups),
        out_specs=(vmem_spec(), any_spec()),
        scratch_shapes=[
            pltpu.VMEM((heads, length, WIDE), F32),
            pltpu.VMEM((2, heads, groups, rows, WIDE), BF16),
            pltpu.SemaphoreType.DMA((2,)),
        ],
        compiler_params=pltpu.CompilerParams(vmem_limit_bytes=VMEM_BYTES),
        cost_estimate=pl.CostEstimate(
            flops=10 * heads * groups * rows * length * WIDE // 2,
            bytes_accessed=8 * heads * length * WIDE,
            transcendentals=0,
        ),
        name="attend_back",
    )(place, span, q, kv, wk, ctx, lse, code_k, doc_q, *dctx)


def norm(v, gain, shift):
    centred = v - jnp.mean(v, -1, keepdims=True)
    inverse = lax.rsqrt(jnp.mean(centred * centred, -1, keepdims=True) + EPS)
    normed = centred * inverse
    return normed * gain + shift, normed, inverse


def norm_back(g, normed, inverse, gain):
    scaled = g * gain
    inward = inverse * (
        scaled
        - jnp.mean(scaled, -1, keepdims=True)
        - normed * jnp.mean(scaled * normed, -1, keepdims=True)
    )
    return inward, jnp.sum(g * normed, 0, keepdims=True), jnp.sum(g, 0, keepdims=True)


def middle_kernel(
    groups, parts, w_col, place, x, cot, vec, w_hbm, *refs
):
    ctx = refs[:groups]
    out, g_hbm, dsum_out, vec_out = refs[groups : groups + 4]
    dctx = refs[groups + 4 : 2 * groups + 4]
    w, g, inner_s, act_s, w_sem, g_sem = refs[2 * groups + 4 :]
    width = x.shape[1]
    share = width // groups

    def w_copy(j):
        return pltpu.make_async_copy(
            w_hbm.at[:, pl.ds(w_col + j * width, width)], w.at[j], w_sem.at[j]
        )

    def g_copy(j):
        return pltpu.make_async_copy(
            g.at[j], g_hbm.at[:, pl.ds(j * width, width)], g_sem.at[j]
        )

    blocks = 1 + 2 * parts
    order = [0] + [i for j in range(parts) for i in (1 + j, 1 + parts + j)]
    for j in order:
        w_copy(j).start()
    srcs = [lax.rem(place[0] + (groups - d), groups) for d in range(groups)]

    def rows_of(s):
        return pl.ds(pl.multiple_of(s * share, HD), share)

    w_copy(0).wait()
    attended = vec[0:1, :]
    for d in range(groups):
        attended = attended + dot(ctx[d][...], w[0, rows_of(srcs[d]), :])
    first, n1, r1 = norm(x[...].astype(F32) + attended, vec[1:2, :], vec[2:3, :])
    low = first.astype(BF16)
    outer = vec[3:4, :] + first
    for j in range(parts):
        w_copy(1 + j).wait()
        w_copy(1 + parts + j).wait()
        inner = dot(low, w[1 + j]) + vec[6 + j : 7 + j, :]
        inner_s[j] = inner
        act = 0.5 * inner * (1.0 + jnp.tanh(GELU_A * (inner + GELU_B * inner * inner * inner)))
        act_low = act.astype(BF16)
        act_s[j] = act_low
        outer = outer + dot(act_low, w[1 + parts + j])
    second, n2, r2 = norm(outer, vec[4:5, :], vec[5:6, :])
    out[...] = second.astype(BF16)
    d_second, dgain2, dshift2 = norm_back(cot[...].astype(F32), n2, r2, vec[4:5, :])
    d_outer = d_second.astype(BF16)
    vec_out[...] = jnp.zeros(vec_out.shape, F32)
    vec_out[4:5, :] = dgain2
    vec_out[5:6, :] = dshift2
    vec_out[3:4, :] = jnp.sum(d_outer.astype(F32), 0, keepdims=True)
    d_first = d_second
    for j in range(parts):
        g[1 + parts + j] = dot_tn(act_s[j], d_outer).astype(BF16)
        g_copy(1 + parts + j).start()
        v = inner_s[j]
        t = jnp.tanh(GELU_A * (v + GELU_B * v * v * v))
        slope = 0.5 * (1.0 + t) + 0.5 * v * (1.0 - t * t) * (
            GELU_A * (1.0 + 3.0 * GELU_B * v * v)
        )
        d_inner = (dot_nt(d_outer, w[1 + parts + j]) * slope).astype(BF16)
        vec_out[6 + j : 7 + j, :] = jnp.sum(d_inner.astype(F32), 0, keepdims=True)
        g[1 + j] = dot_tn(low, d_inner).astype(BF16)
        g_copy(1 + j).start()
        d_first = d_first + dot_nt(d_inner, w[1 + j])
    d_sum, dgain1, dshift1 = norm_back(d_first, n1, r1, vec[1:2, :])
    dsum_out[...] = d_sum
    d_att = d_sum.astype(BF16)
    vec_out[1:2, :] = dgain1
    vec_out[2:3, :] = dshift1
    vec_out[0:1, :] = jnp.sum(d_att.astype(F32), 0, keepdims=True)
    for d in range(groups):
        g[0, rows_of(srcs[d]), :] = dot_tn(ctx[d][...], d_att).astype(BF16)
        dctx[d][...] = dot_nt(d_att, w[0, rows_of(srcs[d]), :]).astype(BF16)
    g_copy(0).start()
    for j in range(blocks):
        g_copy(j).wait()


def middle(place, x, cot, vec, w, ctx, parts, w_col):
    groups = len(ctx)
    rows, width = x.shape
    blocks = 1 + 2 * parts

    def kernel(place_ref, *refs):
        middle_kernel(groups, parts, w_col, place_ref, *refs)

    result = pl.pallas_call(
        kernel,
        out_shape=(
            jax.ShapeDtypeStruct((rows, width), BF16),
            jax.ShapeDtypeStruct((width, blocks * width), BF16),
            jax.ShapeDtypeStruct((rows, width), F32),
            jax.ShapeDtypeStruct((16, width), F32),
        )
        + tuple(jax.ShapeDtypeStruct(c.shape, BF16) for c in ctx),
        in_specs=[smem_spec(), vmem_spec(), vmem_spec(), vmem_spec(), any_spec()]
        + [vmem_spec()] * groups,
        out_specs=(vmem_spec(), any_spec(), vmem_spec(), vmem_spec()) + (vmem_spec(),) * groups,
        scratch_shapes=[
            pltpu.VMEM((blocks, width, width), BF16),
            pltpu.VMEM((blocks, width, width), BF16),
            pltpu.VMEM((parts, rows, width), F32),
            pltpu.VMEM((parts, rows, width), BF16),
            pltpu.SemaphoreType.DMA((blocks,)),
            pltpu.SemaphoreType.DMA((blocks,)),
        ],
        compiler_params=pltpu.CompilerParams(vmem_limit_bytes=VMEM_BYTES),
        cost_estimate=pl.CostEstimate(
            flops=6 * rows * width * width * blocks,
            bytes_accessed=4 * width * width * blocks,
            transcendentals=2 * rows * width * parts,
        ),
        name="middle",
    )(place, x, cot, vec, w, *ctx)
    return result[0], result[1], result[2], result[3], result[4:]


def project_back_kernel(groups, heads, blocks, place, x, w_hbm, flag, dq, *refs):
    dkv = refs[:blocks]
    dx_out, gw_out, bias_out, w, d_all, sem = refs[blocks:]
    rows = x.shape[1]
    cols = w.shape[1]
    half = heads * WIDE
    copy = pltpu.make_async_copy(
        w_hbm.at[:, pl.ds(pl.multiple_of(place[0] * cols, 128), cols)], w, sem
    )
    copy.start()
    for g in range(groups):
        entity = flag[g]
        at = slice(g * rows, (g + 1) * rows)
        for h in range(heads):
            d = dq[h, g].astype(F32)
            d_all[at, h * WIDE : (h + 1) * WIDE] = (d * (1.0 - entity)).astype(BF16)
            d_all[at, half + h * WIDE : half + (h + 1) * WIDE] = (d * entity).astype(BF16)
            total = dkv[0][h, g].astype(F32)
            for p in range(1, blocks):
                total = total + dkv[p][h, g].astype(F32)
            d_all[at, 2 * half + h * WIDE : 2 * half + (h + 1) * WIDE] = total.astype(BF16)
    bias_out[...] = jnp.broadcast_to(
        jnp.sum(d_all[...].astype(F32), 0, keepdims=True), bias_out.shape
    )
    copy.wait()
    for g in range(groups):
        at = slice(g * rows, (g + 1) * rows)
        dx_out[g] = dot_nt(d_all[at, :], w[...]).astype(BF16)
    xs = jnp.concatenate([x[g] for g in range(groups)], 0)
    gw_out[...] = dot_tn(xs, d_all[...]).astype(BF16)


def project_back(place, x, w, flag, dq, dkv, cols):
    groups, rows, width = x.shape
    heads = dq.shape[0]
    blocks = len(dkv)

    def kernel(place_ref, *refs):
        project_back_kernel(groups, heads, blocks, place_ref, *refs)

    return pl.pallas_call(
        kernel,
        out_shape=(
            jax.ShapeDtypeStruct((groups, rows, width), BF16),
            jax.ShapeDtypeStruct((width, cols), BF16),
            jax.ShapeDtypeStruct((8, cols), F32),
        ),
        in_specs=[smem_spec(), vmem_spec(), any_spec(), vmem_spec(), vmem_spec()]
        + [vmem_spec()] * blocks,
        out_specs=(vmem_spec(), vmem_spec(), vmem_spec()),
        scratch_shapes=[
            pltpu.VMEM((width, cols), BF16),
            pltpu.VMEM((groups * rows, cols), BF16),
            pltpu.SemaphoreType.DMA,
        ],
        compiler_params=pltpu.CompilerParams(vmem_limit_bytes=VMEM_BYTES),
        cost_estimate=pl.CostEstimate(
            flops=4 * groups * rows * width * cols, bytes_accessed=4 * width * cols, transcendentals=0
        ),
        name="project_back",
    )(place, x, w, flag, dq, *dkv)


def make_body(groups, cycle):
    blocks = cycle // 2
    heads = HEADS // groups

    def swap_core(v):
        return lax.ppermute(v, "blk", [(i, i ^ 1) for i in range(cycle)])

    def to_block(v, p):
        return lax.ppermute(v, "blk", [(i, i ^ (2 * p)) for i in range(cycle)])

    def shift(v, d):
        return lax.ppermute(v, "head", [(i, (i + d) % groups) for i in range(groups)])

    def total(v):
        bit = 1
        while bit < cycle:
            v = v + lax.ppermute(v, "blk", [(i, i ^ bit) for i in range(cycle)])
            bit *= 2
        bit = 1
        while bit < groups:
            v = v + lax.ppermute(v, "head", [(i, i ^ bit) for i in range(groups)])
            bit *= 2
        return v

    def pick(v, i):
        return lax.dynamic_index_in_dim(v, i, 0, keepdims=False)

    def body(
        hidden,
        entity_flags,
        doc_lengths,
        cotangent,
        query_weight,
        query_bias,
        keyval_weight,
        value_bias,
        output_weight,
        output_bias,
        first_gain,
        first_shift,
        inner_weight,
        inner_bias,
        outer_weight,
        outer_bias,
        second_gain,
        second_shift,
    ):
        micro, own_rows, width = hidden.shape
        hidden_units = inner_bias.shape[0]
        parts = hidden_units // width
        length = own_rows * groups * cycle
        rows = 2 * own_rows
        z = lax.axis_index("head")
        b = lax.axis_index("blk")
        core = lax.rem(b, 2)
        column = b // 2
        place = jnp.stack([z, column, core, b]).astype(jnp.int32)
        everywhere = ("head", "blk")

        both = jnp.stack([hidden, cotangent], 1)
        mine = pick(both, core)
        came = swap_core(pick(both, 1 - core))
        chip = jnp.where(
            core == 0, jnp.concatenate([mine, came], 1), jnp.concatenate([came, mine], 1)
        )
        x = chip[0]
        cot = chip[1]
        xs = [x] + [shift(x, d) for d in range(1, groups)]

        depth = query_weight.shape[0] // (4 * width)
        wq = query_weight.reshape(depth, 2, 2, groups, heads, HD)
        wq = wq.transpose(0, 3, 1, 4, 2, 5).reshape(depth, groups, 4 * heads * HD)
        wkv = keyval_weight.reshape(depth, 2, groups, heads, HD)
        wkv = wkv.transpose(0, 2, 3, 1, 4).reshape(depth, groups, 2 * heads * HD)
        cols = 6 * heads * HD
        w_qkv = jnp.concatenate([wq, wkv], 2).reshape(depth, groups * cols)
        w_in = inner_weight.reshape(depth, width, parts).transpose(0, 2, 1).reshape(depth, hidden_units)
        w_own = jnp.concatenate(
            [
                w_qkv,
                output_weight.reshape(depth, width),
                w_in,
                outer_weight.reshape(depth, hidden_units),
            ],
            1,
        )
        w_all = lax.all_gather(w_own, everywhere, axis=0, tiled=True)

        flags = pick(lax.all_gather(entity_flags, everywhere, axis=1, tiled=True), core)
        lengths = pick(doc_lengths, core)
        count = lengths.shape[0]
        index = jnp.arange(count, dtype=jnp.int32)
        ends = jnp.sum(jnp.where(index[None, :] <= index[:, None], lengths[None, :], 0), 1)
        positions = jnp.arange(length, dtype=jnp.int32)
        docs = jnp.sum((ends[None, :] <= positions[:, None]).astype(jnp.int32), 1)
        docs_seg = docs.reshape(groups, blocks, rows)
        doc_q = lax.dynamic_index_in_dim(docs_seg, column, 1, keepdims=False)
        flag_q = lax.dynamic_index_in_dim(
            flags.reshape(groups, blocks, rows), column, 1, keepdims=False
        ).astype(F32)[..., None]
        code_k = (2 * docs + flags).astype(BF16)[:, None]
        chunk = chunk_of(length)
        firsts = doc_q[:, 0]
        lasts = doc_q[:, rows - 1]
        begin = jnp.sum(jnp.where(index[None, :] < firsts[:, None], lengths[None, :], 0), 1)
        end = jnp.sum(jnp.where(index[None, :] <= lasts[:, None], lengths[None, :], 0), 1)
        span = jnp.stack([begin // chunk, (end + chunk - 1) // chunk], 1).astype(jnp.int32)

        bq = query_bias.astype(F32).reshape(2, 2, groups, heads, HD)
        bq = bq.transpose(2, 0, 3, 1, 4).reshape(groups, 4 * heads * HD)
        bv = value_bias.astype(F32).reshape(groups, heads, 1, HD)
        bv = jnp.concatenate([jnp.zeros_like(bv), bv], 2).reshape(groups, 2 * heads * HD)
        bias = lax.dynamic_slice_in_dim(jnp.concatenate([bq, bv], 1), z, 1, 0)
        q, kv, x_seg = project(place, xs, w_all, bias, flag_q, heads)
        pieces = [kv] + [to_block(kv, p) for p in range(1, blocks)]
        ctx, lse, kv_all, wk_all = attend(place, span, q, pieces, code_k, doc_q.astype(F32))

        ctx_in = [pick(ctx, z)] + [
            shift(pick(ctx, lax.rem(z + d, groups)), d) for d in range(1, groups)
        ]

        vec = jnp.concatenate(
            [
                v.astype(F32).reshape(-1, width)
                for v in (
                    output_bias,
                    first_gain,
                    first_shift,
                    outer_bias,
                    second_gain,
                    second_shift,
                    inner_bias.reshape(width, parts).T,
                )
            ],
            0,
        )
        low_out, g_mid, d_sum, g_vec, d_ctx = middle(
            place, x, cot, vec, w_all, ctx_in, parts, groups * cols
        )
        mid_own = lax.psum_scatter(g_mid, everywhere, scatter_dimension=0, tiled=True).astype(F32)
        vec_sum = total(g_vec)

        d_heads = [d_ctx[0]] + [shift(d_ctx[d], groups - d) for d in range(1, groups)]
        d_heads = [d_heads[0]] + [d_heads[groups - d] for d in range(1, groups)]
        dq, dkv = attend_back(
            place, span, q, kv_all, wk_all, ctx, lse, code_k, doc_q.astype(F32), d_heads
        )
        dkv_in = [dkv[0]] + [to_block(dkv[p], p) for p in range(1, blocks)]
        dx, gw, g_bias = project_back(place, x_seg, w_all, flag_q, dq, dkv_in, cols)

        dx_in = [pick(dx, z)] + [
            shift(pick(dx, lax.rem(z + d, groups)), d) for d in range(1, groups)
        ]
        grad_x = d_sum
        for piece in dx_in:
            grad_x = grad_x + piece.astype(F32)

        halves_g = grad_x.reshape(2, own_rows, width)
        halves_o = low_out.reshape(2, own_rows, width)
        keep_g, send_g = pick(halves_g, core), pick(halves_g, 1 - core)
        keep_o, send_o = pick(halves_o, core), pick(halves_o, 1 - core)
        came_g, came_o = swap_core(send_g), swap_core(send_o)

        def in_order(kept, arrived):
            return jnp.where(core == 0, jnp.stack([kept, arrived]), jnp.stack([arrived, kept]))

        grad_hidden = in_order(keep_g, came_g)
        layer_output = in_order(keep_o, came_o)

        gw = gw.reshape(groups, cycle, depth, cols).transpose(1, 0, 2, 3)
        gw = lax.psum_scatter(gw, "blk", scatter_dimension=0, tiled=True)[0]
        gw = lax.all_to_all(gw, "head", split_axis=0, concat_axis=0, tiled=True).astype(F32)
        grad_query = (
            gw[:, :, : 4 * heads * HD]
            .reshape(groups, depth, 2, heads, 2, HD)
            .transpose(1, 2, 4, 0, 3, 5)
            .reshape(-1)
        )
        grad_keyval = (
            gw[:, :, 4 * heads * HD :]
            .reshape(groups, depth, heads, 2, HD)
            .transpose(1, 3, 0, 2, 4)
            .reshape(-1)
        )
        slot = jnp.arange(groups)[:, None] == z
        bias_sum = total(jnp.where(slot, g_bias[:1], 0.0))
        grad_qbias = (
            bias_sum[:, : 4 * heads * HD]
            .reshape(groups, 2, heads, 2, HD)
            .transpose(1, 3, 0, 2, 4)
            .reshape(4, width)
        )
        grad_vbias = bias_sum[:, 4 * heads * HD :].reshape(groups, heads, 2, HD)[:, :, 1].reshape(width)

        grad_output = mid_own[:, :width].reshape(-1)
        grad_inner = (
            mid_own[:, width : width + hidden_units]
            .reshape(depth, parts, width)
            .transpose(0, 2, 1)
            .reshape(-1)
        )
        grad_outer = mid_own[:, width + hidden_units :].reshape(-1)
        return (
            layer_output,
            grad_hidden,
            grad_query,
            grad_qbias,
            grad_keyval,
            grad_vbias,
            grad_output,
            vec_sum[0],
            vec_sum[1],
            vec_sum[2],
            grad_inner,
            vec_sum[6 : 6 + parts].T.reshape(hidden_units),
            grad_outer,
            vec_sum[3],
            vec_sum[4],
            vec_sum[5],
        )

    return body


def solution(mesh):
    split = P(("head", "blk"))
    tokens = P(None, ("head", "blk"), None)
    return jax.shard_map(
        make_body(mesh.shape["head"], mesh.shape["blk"]),
        mesh=mesh,
        in_specs=(
            tokens,
            P(None, ("head", "blk")),
            P(),
            tokens,
            split,
            P(),
            split,
            P(),
            split,
            P(),
            P(),
            P(),
            split,
            P(),
            split,
            P(),
            P(),
            P(),
        ),
        out_specs=(
            tokens,
            tokens,
            split,
            P(),
            split,
            P(),
            split,
            P(),
            P(),
            P(),
            split,
            P(),
            split,
            P(),
            P(),
            P(),
        ),
        check_vma=False,
    )
```
